32 devices in a mesh: rows: 16 (over z, y, core), tp: 2 (over x).
Axes of the slice: x: 2, y: 2, z: 4, core: 2. Of those that a mesh axis runs over, the one named last changes fastest.
Arguments:
- normed_rows: bfloat16 [4096, 8192], P('rows'), may hold values from -6 to 6
- value_weight: bfloat16 [8192, 1024], P(None, 'tp'), may hold values from -0.0625 to 0.0625
- adapter_a: bfloat16 [32, 8192, 64], P('rows', 'tp'), may hold values from -0.0625 to 0.0625
- adapter_b: bfloat16 [32, 64, 1024], P('rows', None, 'tp'), may hold values from -0.75 to 0.75
- page_table: int32 [32], replicated, may hold values from 0 to 31, as said below
- group_list: int32 [16, 16], replicated, may hold values from 0 to 31, as said below
- seg_len: int32 [16, 16], P('rows'), may hold values from 1 to 32, 256 in all within a row
- kv_len: int32 [16, 256], P('rows'), may hold values from 1 to 32, 4096 in all within a row
- queries: bfloat16 [4096, 8192], P('rows', 'tp'), may hold values from -8 to 8
- new_key: bfloat16 [4096, 1024], P('rows', 'tp'), may hold values from -8 to 8
- cache_keys: bfloat16 [4096, 32, 1024], P('rows', None, 'tp'), may hold values from -8 to 8
- cache_values: bfloat16 [4096, 32, 1024], P('rows', None, 'tp'), may hold values from -6 to 6
Outputs:
- new_value: bfloat16 [4096, 1024], P('rows', 'tp')
- attended: bfloat16 [4096, 8192], P('rows', 'tp')
The draws below stay inside these ranges and needn't reach their ends.
Inputs may be any that keep to these rules, and one draw needn't show every extreme that they name: `page_table`: each adapter has one position; the device of rows index p // 2 stores position p. `group_list`: the 16 adapters of a group are stored on 16 different indices of rows.
All inputs are finite; a program needn't handle non-finite values.
Results may differ from the reference program's by a relative error of at most 0.0048.
Values may be sent and summed in bfloat16 or wider, within the bound.
A program may use at most 128 MiB of HBM per device.

```python
import math
import jax
import jax.numpy as jnp
import numpy as np
from jax import lax

D = 8192
QH = 64
KVH = 8
HEAD = 128
RANK = 64
ROWS_DEV = 256
CACHE = 32
ADP_DEV = 2
GROUPS = 16
ROWS = 4096
ADAPTERS = 32
SLOTS = 16
MOST = 32


def pick_owners(sub_key):
    return jax.random.permutation(sub_key, GROUPS)[:SLOTS]


def page_parts(key):
    order = jax.random.permutation(jax.random.fold_in(key, 21), ADAPTERS).astype(jnp.int32)
    holder = jnp.argsort(order, stable=True).astype(jnp.int32)
    sub_keys = jax.random.split(jax.random.fold_in(key, 22), GROUPS)
    owners = jax.vmap(pick_owners)(sub_keys).astype(jnp.int32)
    local = jax.random.randint(jax.random.fold_in(key, 23), (GROUPS, SLOTS), 0, ADP_DEV).astype(jnp.int32)
    listed = holder[owners * ADP_DEV + local]
    return (order, listed.astype(jnp.int32))


def draw_page_table(key, part):
    order, listed = page_parts(key)
    return order


def draw_group_list(key, part):
    order, listed = page_parts(key)
    return listed


def draw_queries(key, part):
    key = jax.random.fold_in(key, 1)
    base = jnp.clip(jax.random.normal(key, (ROWS, QH, HEAD), jnp.float32), -8.0, 8.0)
    return base.reshape(ROWS, QH * HEAD).astype(jnp.bfloat16)


def draw_cache_keys(key, part):
    key = jax.random.fold_in(key, 2)
    base = jnp.clip(jax.random.normal(key, (ROWS, CACHE, KVH, HEAD), jnp.float32), -8.0, 8.0)
    return base.reshape(ROWS, CACHE, KVH * HEAD).astype(jnp.bfloat16)


def draw_new_key(key, part):
    key = jax.random.fold_in(key, 3)
    base = jnp.clip(jax.random.normal(key, (ROWS, KVH, HEAD), jnp.float32), -8.0, 8.0)
    return base.reshape(ROWS, KVH * HEAD).astype(jnp.bfloat16)


def shard_levels(own_key, extent, cuts, low, largest):
    def one(dim, shards_of):
        draws = jax.random.uniform(jax.random.fold_in(jax.random.fold_in(own_key, 6), dim), (shards_of,), jnp.float32, low / len(cuts), largest / len(cuts))
        return jnp.repeat(jnp.exp(draws), extent[dim] // shards_of).reshape((-1,) + (1,) * (len(extent) - dim - 1))

    loudness = one(*cuts[0])
    for cut in cuts[1:]:
        loudness = loudness * one(*cut)
    return loudness


def length_profile(count, total, bound, skew):
    loads = [(1 << 20) // math.isqrt(standing ** skew) + 1 for standing in range(2, count + 1)]
    spare, given = total - bound - (count - 1), [1] * (count - 1)
    while spare > 0:
        candidates = [i for i in range(count - 1) if given[i] < bound]
        mass, left = sum([loads[i] for i in candidates]), spare
        for i in candidates:
            extra = min(bound - given[i], max(1, left * loads[i] // mass), spare)
            given[i] = given[i] + extra
            spare = spare - extra
    return np.array([bound] + given)


def ragged_sizes(own_key, count, total, reach, slope):
    if count == 2:
        one = jax.random.randint(own_key, (), max(1, total - reach), min(reach, total - 1) + 1)
        return jnp.stack([one, total - one])
    tallies = jnp.asarray(length_profile(count, total, reach, slope), jnp.int32)
    twos = (count - 1) // 2
    giver, receiver = tallies[1:1 + 2 * twos:2], tallies[2:2 + 2 * twos:2]
    slack = jnp.minimum(giver - 1, reach - receiver)
    moved = jax.random.randint(jax.random.fold_in(own_key, 1), (twos,), 0, 1 << 20) % (slack + 1)
    tallies = tallies.at[1:1 + 2 * twos:2].set(giver - moved).at[2:2 + 2 * twos:2].set(receiver + moved)
    return tallies[jax.random.permutation(jax.random.fold_in(own_key, 2), count)]


def normal_values(key, dims, deviation, reach, cuts=(), kind=jnp.bfloat16):
    entries = jax.random.normal(key, dims, jnp.float32) * deviation
    if len(cuts) > 0:
        entries = shard_levels(key, dims, cuts, -0.22, 0.18) * entries
    return jnp.clip(entries, min=-reach, max=reach).astype(kind)


def setup_inputs(seed: int = 0) -> dict:
    seeds = jax.random.split(jax.random.key(seed), 13)
    normed_rows = normal_values(seeds[0], (ROWS, D), 1.0, 6.0, ((0, 16),))
    value_weight = normal_values(seeds[1], (D, KVH * HEAD), D ** -0.5, 0.0625, ((1, 2),))
    adapter_a = normal_values(seeds[2], (ADAPTERS, D, RANK), D ** -0.5, 0.0625, ((0, 16), (1, 2)))
    adapter_b = normal_values(seeds[3], (ADAPTERS, RANK, KVH * HEAD), RANK ** -0.5, 0.75, ((0, 16), (2, 2)))
    page_table = draw_page_table(jax.random.fold_in(seeds[12], 71), 0)
    group_list = draw_group_list(jax.random.fold_in(seeds[12], 71), 0)
    seg_len = jax.vmap(lambda own: ragged_sizes(own, SLOTS, ROWS_DEV, MOST, 1))(jax.random.split(seeds[6], GROUPS)).reshape((GROUPS, SLOTS)).astype(jnp.int32)
    kv_len = jax.vmap(lambda own: ragged_sizes(own, ROWS_DEV, ROWS_DEV * CACHE // 2, CACHE, 2))(jax.random.split(seeds[7], GROUPS)).reshape((GROUPS, ROWS_DEV)).astype(jnp.int32)
    queries = draw_queries(jax.random.fold_in(seeds[12], 71), 0)
    new_key = draw_new_key(jax.random.fold_in(seeds[12], 71), 0)
    cache_keys = draw_cache_keys(jax.random.fold_in(seeds[12], 71), 0)
    cache_values = normal_values(seeds[11], (ROWS, CACHE, KVH * HEAD), 1.0, 6.0, ((0, 16), (2, 2)))
    return {"normed_rows": normed_rows, "value_weight": value_weight, "adapter_a": adapter_a, "adapter_b": adapter_b, "page_table": page_table, "group_list": group_list, "seg_len": seg_len, "kv_len": kv_len, "queries": queries, "new_key": new_key, "cache_keys": cache_keys, "cache_values": cache_values}


def segment_rows(lens, rows_count):
    ends = jnp.cumsum(lens).astype(jnp.int32)
    rowpos = jnp.arange(rows_count, dtype=jnp.int32)
    return lax.optimization_barrier(jnp.sum((rowpos[:, None] >= ends[None, :]).astype(jnp.int32), axis=1)).astype(jnp.int32)

def attend(query_rows, key_new, keys, values, value_new, lengths):
    count = query_rows.shape[0]
    heads_kv = key_new.shape[1] // HEAD
    group = query_rows.shape[1] // key_new.shape[1]
    scale = 1.0 / math.sqrt(HEAD)
    q_four = query_rows.reshape(count, heads_kv, group, HEAD).astype(jnp.float32)
    k_four = keys.reshape(count, -1, heads_kv, HEAD).astype(jnp.float32)
    v_four = values.reshape(count, -1, heads_kv, HEAD).astype(jnp.float32)
    k_own = key_new.reshape(count, heads_kv, HEAD).astype(jnp.float32)
    v_own = value_new.reshape(count, heads_kv, HEAD).astype(jnp.float32)
    score = jnp.einsum('rhgd,rchd->rhgc', q_four, k_four) * scale
    own = jnp.einsum('rhgd,rhd->rhg', q_four, k_own) * scale
    valid = (jnp.arange(keys.shape[1], dtype=jnp.int32)[None, :] < lengths[:, None])[:, None, None, :]
    top = jnp.maximum(lax.optimization_barrier(jnp.max(jnp.where(valid, score, -jnp.inf), axis=-1)), own)
    expd = jnp.where(valid, jnp.exp(score - top[..., None]), 0.0)
    exp_own = jnp.exp(own - top)
    total = lax.optimization_barrier(jnp.sum(expd, axis=-1)) + exp_own
    weight = lax.optimization_barrier(expd.astype(jnp.bfloat16)).astype(jnp.float32)
    weight_own = lax.optimization_barrier(exp_own.astype(jnp.bfloat16)).astype(jnp.float32)
    context = jnp.einsum('rhgc,rchd->rhgd', weight, v_four) + weight_own[..., None] * v_own[:, :, None, :]
    return (context / total[..., None]).astype(jnp.bfloat16).reshape(count, -1)

def reference(normed_rows, value_weight, adapter_a, adapter_b, page_table, group_list, seg_len, kv_len, queries, new_key, cache_keys, cache_values):
    width_kv = KVH * HEAD

    def one_group(items):
        rows_x, rows_q, rows_k, rows_ck, rows_cv, lens_kv, lens_seg, listed = items
        segment = segment_rows(lens_seg, ROWS_DEV)
        stored = page_table[listed[segment]]
        a_rows = adapter_a[stored].astype(jnp.float32)
        low = jnp.einsum('rd,rdk->rk', rows_x.astype(jnp.float32), a_rows)
        low = lax.optimization_barrier(low.astype(jnp.bfloat16)).astype(jnp.float32)
        b_rows = adapter_b[stored].astype(jnp.float32)
        delta = jnp.einsum('rk,rkv->rv', low, b_rows)
        delta = lax.optimization_barrier(delta.astype(jnp.bfloat16)).astype(jnp.float32)
        base = jnp.dot(rows_x, value_weight, preferred_element_type=jnp.float32)
        value_new = (base + delta).astype(jnp.bfloat16)
        result = attend(rows_q, rows_k, rows_ck, rows_cv, value_new, lens_kv)
        return (value_new, result)
    stacked = (normed_rows.reshape(GROUPS, ROWS_DEV, D), queries.reshape(GROUPS, ROWS_DEV, QH * HEAD), new_key.reshape(GROUPS, ROWS_DEV, width_kv), cache_keys.reshape(GROUPS, ROWS_DEV, CACHE, width_kv), cache_values.reshape(GROUPS, ROWS_DEV, CACHE, width_kv), kv_len, seg_len, group_list)
    new_value, attended = lax.map(one_group, stacked)
    return (new_value.reshape(ROWS, width_kv), attended.reshape(ROWS, QH * HEAD))
```

```python
import functools
import math

import jax
import jax.numpy as jnp
from jax import lax
from jax.experimental import pallas as pl
from jax.experimental.pallas import tpu as pltpu
from jax.sharding import Mesh, PartitionSpec as P

HEAD = 128
BLOCK = 16
OFF = -1e30


def attend_kernel(heads_kv, group, scale, q_ref, kn_ref, k_ref, v_ref, col_ref, diag_ref, ctx_ref, own_ref):
    rows = q_ref.shape[0]
    cache = k_ref.shape[1]
    for h in range(heads_kv):
        lanes = pl.ds(h * HEAD, HEAD)
        q = jnp.concatenate(
            [q_ref[:, pl.ds((h * group + g) * HEAD, HEAD)] for g in range(group)], axis=0
        )
        k = k_ref[:, :, lanes].reshape(rows * cache, HEAD)
        v = v_ref[:, :, lanes].reshape(rows * cache, HEAD)
        score = lax.dot_general(q, k, (((1,), (1,)), ((), ())), preferred_element_type=jnp.float32)
        score = score * scale + (diag_ref[...] + col_ref[0])
        kn = kn_ref[:, lanes].astype(jnp.float32)
        kn = jnp.concatenate([kn] * group, axis=0)
        own = jnp.sum(q.astype(jnp.float32) * kn, axis=1, keepdims=True) * scale
        top = jnp.maximum(jnp.max(score, axis=1, keepdims=True), own)
        e = jnp.exp(score - top)
        e_own = jnp.exp(own - top)
        total = jnp.sum(e, axis=1, keepdims=True) + e_own
        ctx = jnp.dot(e.astype(jnp.bfloat16), v, preferred_element_type=jnp.float32) / total
        own_w = e_own.astype(jnp.bfloat16).astype(jnp.float32) / total
        for g in range(group):
            part = slice(g * rows, (g + 1) * rows)
            ctx_ref[:, pl.ds((h * group + g) * HEAD, HEAD)] = ctx[part]
            own_ref[:, pl.ds(h * group + g, 1)] = own_w[part]


def attend(queries, new_key, cache_keys, cache_values, lengths):
    rows, width = queries.shape
    cache = cache_keys.shape[1]
    heads_kv = new_key.shape[1] // HEAD
    group = width // new_key.shape[1]
    blocks = rows // BLOCK
    wide = BLOCK * cache
    valid = jnp.arange(cache, dtype=jnp.int32)[None, :] < lengths[:, None]
    col = jnp.where(valid, 0.0, OFF).astype(jnp.float32).reshape(blocks, 1, wide)
    diag = jnp.where(
        (jnp.arange(group * BLOCK, dtype=jnp.int32) % BLOCK)[:, None]
        == (jnp.arange(wide, dtype=jnp.int32) // cache)[None, :],
        0.0,
        OFF,
    ).astype(jnp.float32)
    return pl.pallas_call(
        functools.partial(attend_kernel, heads_kv, group, 1.0 / math.sqrt(HEAD)),
        grid=(blocks,),
        in_specs=[
            pl.BlockSpec((BLOCK, width), lambda i: (i, 0)),
            pl.BlockSpec((BLOCK, new_key.shape[1]), lambda i: (i, 0)),
            pl.BlockSpec((BLOCK, cache, new_key.shape[1]), lambda i: (i, 0, 0)),
            pl.BlockSpec((BLOCK, cache, new_key.shape[1]), lambda i: (i, 0, 0)),
            pl.BlockSpec((1, 1, wide), lambda i: (i, 0, 0)),
            pl.BlockSpec((group * BLOCK, wide), lambda i: (0, 0)),
        ],
        out_specs=[
            pl.BlockSpec((BLOCK, width), lambda i: (i, 0)),
            pl.BlockSpec((BLOCK, heads_kv * group), lambda i: (i, 0)),
        ],
        out_shape=[
            jax.ShapeDtypeStruct((rows, width), jnp.float32),
            jax.ShapeDtypeStruct((rows, heads_kv * group), jnp.float32),
        ],
        compiler_params=pltpu.CompilerParams(vmem_limit_bytes=24 * 1024 * 1024),
        cost_estimate=pl.CostEstimate(
            flops=4 * rows * group * heads_kv * wide * HEAD,
            bytes_accessed=2 * 2 * cache_keys.size + 6 * queries.size,
            transcendentals=rows * group * heads_kv * wide,
        ),
        name="attend_cache",
    )(queries, new_key, cache_keys, cache_values, col, diag)


def finish_kernel(order, most, group, low_ref, mask_ref, b_ref, place_ref, base_ref, ctx_ref, own_ref, nv_ref, att_ref, delta):
    @pl.when(pl.program_id(0) == 0)
    def _():
        per = low_ref.shape[2] // most
        for i, o in enumerate(order):
            at = pl.ds((i % per) * most, most)
            low = low_ref[i // per, 0, at, :]
            for t in range(1, low_ref.shape[1]):
                low = low + low_ref[i // per, t, at, :]
            low = (low * mask_ref[pl.ds(o, 1), :]).astype(jnp.bfloat16)
            out = jnp.dot(low, b_ref[o], preferred_element_type=jnp.float32)
            delta[pl.ds(i * most, most), :] = out.astype(jnp.bfloat16).astype(jnp.float32)

    rows = jnp.dot(place_ref[...], delta[...].astype(jnp.bfloat16), preferred_element_type=jnp.float32)
    value = (base_ref[...] + rows).astype(jnp.bfloat16)
    nv_ref[...] = value
    value = value.astype(jnp.float32)
    for i in range(own_ref.shape[1]):
        lanes = pl.ds(i * HEAD, HEAD)
        h = i // group
        att_ref[:, lanes] = (
            ctx_ref[:, lanes] + own_ref[:, pl.ds(i, 1)] * value[:, h * HEAD : (h + 1) * HEAD]
        ).astype(jnp.bfloat16)


def finish(order, most, low, mask, b_all, place, base, ctx, own):
    rows, width = ctx.shape
    cols = base.shape[1]
    step = rows // 4
    whole = lambda a: pl.BlockSpec(a.shape, lambda i: (0,) * a.ndim)
    split = lambda a: pl.BlockSpec((step, a.shape[1]), lambda i: (i, 0))
    return pl.pallas_call(
        functools.partial(finish_kernel, order, most, width // cols),
        grid=(4,),
        in_specs=[whole(low), whole(mask), whole(b_all), split(place), split(base), split(ctx), split(own)],
        out_specs=[split(base), split(ctx)],
        out_shape=[
            jax.ShapeDtypeStruct((rows, cols), jnp.bfloat16),
            jax.ShapeDtypeStruct((rows, width), jnp.bfloat16),
        ],
        scratch_shapes=[pltpu.VMEM((place.shape[1], cols), jnp.float32)],
        compiler_params=pltpu.CompilerParams(vmem_limit_bytes=40 * 1024 * 1024),
        cost_estimate=pl.CostEstimate(
            flops=4 * rows * place.shape[1] * cols, bytes_accessed=6 * rows * width, transcendentals=0
        ),
        name="finish_rows",
    )(low, mask, b_all, place, base, ctx, own)


def body(
    normed_rows,
    value_weight,
    adapter_a,
    adapter_b,
    page_table,
    group_list,
    seg_len,
    kv_len,
    queries,
    new_key,
    cache_keys,
    cache_values,
):
    tp_index = lax.axis_index("tp")
    tps = lax.axis_size("tp")
    lines, columns = lax.axis_size("line"), lax.axis_size("slab")
    groups = lines * columns
    me = lax.axis_index("line") * columns + lax.axis_index("slab")
    rows_count = normed_rows.shape[0]
    part = normed_rows.shape[1] // tps
    per_owner, _, rank = adapter_a.shape
    adapters_count = page_table.shape[0]
    lens = seg_len[0]
    slots = lens.shape[0]
    most = 2 * rows_count // slots

    down = adapter_a.transpose(0, 2, 1).reshape(per_owner * rank, part)
    down = lax.all_gather(down, "line")
    up = lax.all_gather(adapter_b.reshape(per_owner * rank, -1), ("line", "slab"))

    ends = jnp.cumsum(lens)
    starts = ends - lens
    rowpos = jnp.arange(rows_count, dtype=jnp.int32)
    in_segment = (rowpos[:, None] >= starts[None, :]) & (rowpos[:, None] < ends[None, :])
    listed = lax.dynamic_index_in_dim(group_list, me, 0, keepdims=False)
    positions = jnp.sum(
        jnp.where(
            listed[:, None] == jnp.arange(adapters_count, dtype=jnp.int32)[None, :],
            page_table[None, :],
            0,
        ),
        axis=1,
    )
    owners = positions // per_owner
    local = positions % per_owner
    place_of = ((owners % columns) * lines + owners // columns) * most - starts
    target = rowpos + jnp.sum(jnp.where(in_segment, place_of[None, :], 0), axis=1)
    spots = jnp.arange(groups * most, dtype=jnp.int32)
    placing = (spots[:, None] == target[None, :]).astype(jnp.bfloat16)
    taking = (target[:, None] == spots[None, :]).astype(jnp.bfloat16)
    owner_hit = jnp.arange(groups, dtype=jnp.int32)[:, None] == owners[None, :]
    which = jnp.sum(jnp.where(owner_hit, local[None, :], 0), axis=1)
    mask = (
        which[:, None] == (jnp.arange(per_owner * rank, dtype=jnp.int32) // rank)[None, :]
    ).astype(jnp.float32)

    x_part = lax.dynamic_slice_in_dim(normed_rows, tp_index * part, part, 1)
    placed = jnp.dot(placing, x_part, preferred_element_type=jnp.float32).astype(jnp.bfloat16)
    arrived = lax.all_to_all(
        placed.reshape(columns, lines * most, part), "slab", split_axis=0, concat_axis=0, tiled=True
    )
    base = jnp.dot(normed_rows, value_weight, preferred_element_type=jnp.float32)
    ctx, own = attend(queries, new_key, cache_keys, cache_values, kv_len[0])

    low = jnp.stack(
        [
            jnp.einsum(
                "smd,nd->smn",
                arrived[:, z * most : (z + 1) * most],
                down[z],
                preferred_element_type=jnp.float32,
            )
            for z in range(lines)
        ],
        axis=1,
    ).reshape(columns, 1, lines * most, per_owner * rank)
    low = jnp.broadcast_to(low, (columns, tps) + low.shape[2:])
    low = lax.all_to_all(
        low.reshape((columns * tps,) + low.shape[2:]),
        ("slab", "tp"),
        split_axis=0,
        concat_axis=0,
        tiled=True,
    ).reshape(low.shape)
    order = [z * columns + s for s in range(columns) for z in range(lines)]
    return tuple(finish(order, most, low, mask, up, taking, base, ctx, own))


def solution(mesh):
    rows, tps = mesh.shape["rows"], mesh.shape["tp"]
    slab = 2 * math.isqrt(rows // 4)
    split = Mesh(mesh.devices.reshape(rows // slab, slab, tps), ("line", "slab", "tp"))
    pair = ("line", "slab")
    return jax.shard_map(
        body,
        mesh=split,
        in_specs=(
            P(pair, None),
            P(None, "tp"),
            P(pair, "tp", None),
            P(pair, None, "tp"),
            P(),
            P(),
            P(pair, None),
            P(pair, None),
            P(pair, "tp"),
            P(pair, "tp"),
            P(pair, None, "tp"),
            P(pair, None, "tp"),
        ),
        out_specs=(P(pair, "tp"), P(pair, "tp")),
        check_vma=False,
    )
```

```python
import functools
import math

import jax
import jax.numpy as jnp
from jax import lax
from jax.experimental import pallas as pl
from jax.experimental.pallas import tpu as pltpu
from jax.sharding import Mesh, PartitionSpec as P

HEAD = 128
BLOCK = 16
OFF = -1e30


def attend_kernel(heads_kv, group, scale, q_ref, kn_ref, k_ref, v_ref, col_ref, diag_ref, ctx_ref, own_ref):
    rows = q_ref.shape[0]
    cache = k_ref.shape[1]
    for h in range(heads_kv):
        lanes = pl.ds(h * HEAD, HEAD)
        q = jnp.concatenate(
            [q_ref[:, pl.ds((h * group + g) * HEAD, HEAD)] for g in range(group)], axis=0
        )
        k = k_ref[:, :, lanes].reshape(rows * cache, HEAD)
        v = v_ref[:, :, lanes].reshape(rows * cache, HEAD)
        score = lax.dot_general(q, k, (((1,), (1,)), ((), ())), preferred_element_type=jnp.float32)
        score = score * scale + (diag_ref[...] + col_ref[0])
        kn = kn_ref[:, lanes].astype(jnp.float32)
        kn = jnp.concatenate([kn] * group, axis=0)
        own = jnp.sum(q.astype(jnp.float32) * kn, axis=1, keepdims=True) * scale
        top = jnp.maximum(jnp.max(score, axis=1, keepdims=True), own)
        e = jnp.exp(score - top)
        e_own = jnp.exp(own - top)
        total = jnp.sum(e, axis=1, keepdims=True) + e_own
        ctx = jnp.dot(e.astype(jnp.bfloat16), v, preferred_element_type=jnp.float32) / total
        own_w = e_own.astype(jnp.bfloat16).astype(jnp.float32) / total
        for g in range(group):
            part = slice(g * rows, (g + 1) * rows)
            ctx_ref[:, pl.ds((h * group + g) * HEAD, HEAD)] = ctx[part]
            own_ref[:, pl.ds(h * group + g, 1)] = own_w[part]


def attend(queries, new_key, cache_keys, cache_values, lengths):
    rows, width = queries.shape
    cache = cache_keys.shape[1]
    heads_kv = new_key.shape[1] // HEAD
    group = width // new_key.shape[1]
    blocks = rows // BLOCK
    wide = BLOCK * cache
    valid = jnp.arange(cache, dtype=jnp.int32)[None, :] < lengths[:, None]
    col = jnp.where(valid, 0.0, OFF).astype(jnp.float32).reshape(blocks, 1, wide)
    diag = jnp.where(
        (jnp.arange(group * BLOCK, dtype=jnp.int32) % BLOCK)[:, None]
        == (jnp.arange(wide, dtype=jnp.int32) // cache)[None, :],
        0.0,
        OFF,
    ).astype(jnp.float32)
    return pl.pallas_call(
        functools.partial(attend_kernel, heads_kv, group, 1.0 / math.sqrt(HEAD)),
        grid=(blocks,),
        in_specs=[
            pl.BlockSpec((BLOCK, width), lambda i: (i, 0)),
            pl.BlockSpec((BLOCK, new_key.shape[1]), lambda i: (i, 0)),
            pl.BlockSpec((BLOCK, cache, new_key.shape[1]), lambda i: (i, 0, 0)),
            pl.BlockSpec((BLOCK, cache, new_key.shape[1]), lambda i: (i, 0, 0)),
            pl.BlockSpec((1, 1, wide), lambda i: (i, 0, 0)),
            pl.BlockSpec((group * BLOCK, wide), lambda i: (0, 0)),
        ],
        out_specs=[
            pl.BlockSpec((BLOCK, width), lambda i: (i, 0)),
            pl.BlockSpec((BLOCK, heads_kv * group), lambda i: (i, 0)),
        ],
        out_shape=[
            jax.ShapeDtypeStruct((rows, width), jnp.float32),
            jax.ShapeDtypeStruct((rows, heads_kv * group), jnp.float32),
        ],
        compiler_params=pltpu.CompilerParams(vmem_limit_bytes=24 * 1024 * 1024),
        cost_estimate=pl.CostEstimate(
            flops=4 * rows * group * heads_kv * wide * HEAD,
            bytes_accessed=2 * 2 * cache_keys.size + 6 * queries.size,
            transcendentals=rows * group * heads_kv * wide,
        ),
        name="attend_cache",
    )(queries, new_key, cache_keys, cache_values, col, diag)


def finish_kernel(group, delta_ref, place_ref, base_ref, ctx_ref, own_ref, nv_ref, att_ref):
    rows = jnp.dot(place_ref[...], delta_ref[...], preferred_element_type=jnp.float32)
    value = (base_ref[...] + rows).astype(jnp.bfloat16)
    nv_ref[...] = value
    value = value.astype(jnp.float32)
    for i in range(own_ref.shape[1]):
        lanes = pl.ds(i * HEAD, HEAD)
        h = i // group
        att_ref[:, lanes] = (
            ctx_ref[:, lanes] + own_ref[:, pl.ds(i, 1)] * value[:, h * HEAD : (h + 1) * HEAD]
        ).astype(jnp.bfloat16)


def finish(delta, place, base, ctx, own):
    rows, width = ctx.shape
    cols = base.shape[1]
    step = rows // 4
    split = lambda a: pl.BlockSpec((step, a.shape[1]), lambda i: (i, 0))
    return pl.pallas_call(
        functools.partial(finish_kernel, width // cols),
        grid=(4,),
        in_specs=[
            pl.BlockSpec(delta.shape, lambda i: (0, 0)),
            split(place),
            split(base),
            split(ctx),
            split(own),
        ],
        out_specs=[split(base), split(ctx)],
        out_shape=[
            jax.ShapeDtypeStruct((rows, cols), jnp.bfloat16),
            jax.ShapeDtypeStruct((rows, width), jnp.bfloat16),
        ],
        compiler_params=pltpu.CompilerParams(vmem_limit_bytes=32 * 1024 * 1024),
        cost_estimate=pl.CostEstimate(
            flops=4 * rows * place.shape[1] * cols, bytes_accessed=6 * rows * width, transcendentals=0
        ),
        name="finish_rows",
    )(delta, place, base, ctx, own)


def body(
    normed_rows,
    value_weight,
    adapter_a,
    adapter_b,
    page_table,
    group_list,
    seg_len,
    kv_len,
    queries,
    new_key,
    cache_keys,
    cache_values,
):
    tp_index = lax.axis_index("tp")
    tps = lax.axis_size("tp")
    lines, columns = lax.axis_size("line"), lax.axis_size("slab")
    groups = lines * columns
    me = lax.axis_index("line") * columns + lax.axis_index("slab")
    rows_count = normed_rows.shape[0]
    part = normed_rows.shape[1] // tps
    per_owner, _, rank = adapter_a.shape
    adapters_count = page_table.shape[0]
    lens = seg_len[0]
    slots = lens.shape[0]
    most = 2 * rows_count // slots

    down = adapter_a.transpose(0, 2, 1).reshape(per_owner * rank, part)
    maps = jnp.concatenate([down, adapter_b.reshape(per_owner * rank, -1)], axis=1)
    maps = lax.all_gather(maps, "line")

    ends = jnp.cumsum(lens)
    starts = ends - lens
    rowpos = jnp.arange(rows_count, dtype=jnp.int32)
    in_segment = (rowpos[:, None] >= starts[None, :]) & (rowpos[:, None] < ends[None, :])
    positions = jnp.sum(
        jnp.where(
            group_list[:, :, None] == jnp.arange(adapters_count, dtype=jnp.int32),
            page_table,
            0,
        ),
        axis=2,
    )
    held = positions // per_owner
    local = positions % per_owner
    owners = lax.dynamic_index_in_dim(held, me, 0, keepdims=False)
    place_of = ((owners % columns) * lines + owners // columns) * most - starts
    target = rowpos + jnp.sum(jnp.where(in_segment, place_of[None, :], 0), axis=1)
    spots = jnp.arange(groups * most, dtype=jnp.int32)
    placing = (spots[:, None] == target[None, :]).astype(jnp.bfloat16)
    taking = (target[:, None] == spots[None, :]).astype(jnp.bfloat16)
    hit = held[:, None, :] == jnp.arange(groups, dtype=jnp.int32)[None, :, None]
    which = jnp.sum(jnp.where(hit, local[:, None, :], 0), axis=2)
    which = which.reshape(lines, columns, lines, columns)
    which = lax.dynamic_index_in_dim(which, lax.axis_index("line"), 0, keepdims=False)
    which = lax.dynamic_index_in_dim(which, lax.axis_index("slab"), 2, keepdims=False)
    chosen = (
        which[:, :, None, None] == (jnp.arange(per_owner * rank, dtype=jnp.int32) // rank)
    ).astype(jnp.float32)

    x_part = lax.dynamic_slice_in_dim(normed_rows, tp_index * part, part, 1)
    placed = jnp.dot(placing, x_part, preferred_element_type=jnp.float32).astype(jnp.bfloat16)
    arrived = lax.all_to_all(
        placed.reshape(columns, lines * most, part), "slab", split_axis=0, concat_axis=0, tiled=True
    )
    base = jnp.dot(normed_rows, value_weight, preferred_element_type=jnp.float32)
    ctx, own = attend(queries, new_key, cache_keys, cache_values, kv_len[0])

    low = jnp.stack(
        [
            jnp.einsum(
                "smd,nd->smn",
                arrived[:, z * most : (z + 1) * most],
                maps[z, :, :part],
                preferred_element_type=jnp.float32,
            )
            for z in range(lines)
        ],
        axis=1,
    )
    total = low
    for hop in range(1, tps):
        total = total + lax.ppermute(low, "tp", [(t, (t + hop) % tps) for t in range(tps)])
    total = (total * chosen).astype(jnp.bfloat16)
    delta = jnp.stack(
        [
            jnp.einsum(
                "smn,nc->smc", total[:, z], maps[z, :, part:], preferred_element_type=jnp.float32
            ).astype(jnp.bfloat16)
            for z in range(lines)
        ],
        axis=1,
    ).reshape(columns, lines * most, -1)
    delta = lax.all_to_all(delta, "slab", split_axis=0, concat_axis=0, tiled=True)
    return tuple(finish(delta.reshape(groups * most, -1), taking, base, ctx, own))


def solution(mesh):
    rows, tps = mesh.shape["rows"], mesh.shape["tp"]
    slab = 2 * math.isqrt(rows // 4)
    split = Mesh(mesh.devices.reshape(rows // slab, slab, tps), ("line", "slab", "tp"))
    pair = ("line", "slab")
    return jax.shard_map(
        body,
        mesh=split,
        in_specs=(
            P(pair, None),
            P(None, "tp"),
            P(pair, "tp", None),
            P(pair, None, "tp"),
            P(),
            P(),
            P(pair, None),
            P(pair, None),
            P(pair, "tp"),
            P(pair, "tp"),
            P(pair, None, "tp"),
            P(pair, None, "tp"),
        ),
        out_specs=(P(pair, "tp"), P(pair, "tp")),
        check_vma=False,
    )
```
